32 devices in a mesh: grp: 2 (over core), lat: 8 (over z, y), lon: 2 (over x).
Axes of the slice: x: 2, y: 2, z: 4, core: 2. Of those that a mesh axis runs over, the one named last changes fastest.
Arguments:
- control: float32 [64, 320, 1440], P('lon', ('grp', 'lat'))
- spectra: float32 [24, 64, 721], P(None, 'lon')
- band_starts: int32 [40], replicated, may hold values from 0 to 319, as said below
- band_spectrum: int32 [40], replicated, may hold values from 0 to 23, as said below
- shifts: int32 [2], replicated, may hold values from 1 to 9, as said below
- traj_start: bfloat16 [64, 320, 1440], P(None, ('grp', 'lat'), 'lon'), may hold values from -6 to 6
- traj_next: bfloat16 [64, 320, 1440], P(None, ('grp', 'lat'), 'lon'), may hold values from -6 to 6
- query_weight: bfloat16 [64, 256], replicated, may hold values from -0.75 to 0.75
- key_weight: bfloat16 [64, 256], replicated, may hold values from -0.75 to 0.75
- value_weight: bfloat16 [64, 256], replicated, may hold values from -0.75 to 0.75
- out_weight: bfloat16 [256, 64], replicated, may hold values from -0.75 to 0.75
- head_scale: float32 [4], replicated, may hold values from 2 to 12
- innov_one: float32 [64, 320, 1440], P(None, ('grp', 'lat'), 'lon'), may hold values from -6 to 6
- innov_two: float32 [64, 320, 1440], P(None, ('grp', 'lat'), 'lon'), may hold values from -6 to 6
- obs_weight_one: float32 [64, 320, 1440], P(None, ('grp', 'lat'), 'lon')
- obs_weight_two: float32 [64, 320, 1440], P(None, ('grp', 'lat'), 'lon')
- grad_prev: float32 [64, 320, 1440], P('lon', ('grp', 'lat'))
- dir_prev: float32 [64, 320, 1440], P('lon', ('grp', 'lat')), may hold values from -6 to 6
Outputs:
- gradient: float32 [64, 320, 1440], P('lon', ('grp', 'lat'))
- direction: float32 [64, 320, 1440], P('lon', ('grp', 'lat'))
- cost_value: float32 [], replicated
The draws below stay inside these ranges and needn't reach their ends.
Inputs may be any that keep to these rules, and one draw needn't show every extreme that they name: Strictly increasing; the first is 0 and the last is 319; band b holds the rows from band_starts[b] up to the next start. `band_spectrum`: every entry of the table is used by some band. `shifts`: one of the two offsets is 9.
All inputs are finite; a program needn't handle non-finite values.
Results may differ from the reference program's by a relative error of at most 0.0025.
Values may be sent and summed in bfloat16 or wider, within the bound.
A program may use at most 320 MiB of HBM per device.

```python
import math
import jax
import jax.numpy as jnp
from jax import lax

FIELDS = 64
LON = 1440
NK = 721
LAT = 320
WIN = 10
HEADS = 4
HEAD = 64
NBANDS = 40
NSPEC = 24


def spread(key, shape, low, high):
    return jnp.exp(jax.random.uniform(key, shape, jnp.float32, math.log(low), math.log(high)))


def ramp_rows():
    latitude = jnp.arange(LAT, dtype=jnp.float32)
    return jnp.exp(math.log(3.0) * latitude / max(LAT - 1, 1))


def layered_field(key, factor):
    keys = jax.random.split(key, 5)
    base = jax.random.normal(keys[0], (FIELDS, LAT, LON), jnp.float32)
    row_scale = ramp_rows() * spread(keys[2], (LAT,), 0.4, 1.3)
    col_scale = spread(keys[3], (LON,), 0.5, 1.6)
    chan_scale = spread(keys[4], (FIELDS,), 0.5, 1.6)
    return factor * base * chan_scale[:, None, None] * row_scale[None, :, None] * col_scale[None, None, :]


def obs_field(key):
    cells = spread(key, (FIELDS, LAT, LON), 0.5, 2.0)
    return cells * ramp_rows()[None, :, None]


def draw_control(key, part):
    return layered_field(jax.random.fold_in(key, 11), 1.0)


def draw_grad_prev(key, part):
    return layered_field(jax.random.fold_in(key, 12), 1.4)


def draw_obs_weight_one(key, part):
    return obs_field(jax.random.fold_in(key, 13))


def draw_obs_weight_two(key, part):
    return obs_field(jax.random.fold_in(key, 14))


def draw_spectra(key, part):
    inner = jax.random.fold_in(key, 19)
    wave = jnp.arange(NK, dtype=jnp.float32)
    redden = 4.0 / (1.0 + wave / 48.0)
    rough = spread(inner, (NSPEC, FIELDS, NK), 0.5, 2.0)
    return rough * redden[None, None, :]


def draw_band_starts(key, part):
    order = jax.random.permutation(jax.random.fold_in(key, 15), LAT - 2).astype(jnp.int32) + 1
    middle = jnp.sort(order[:NBANDS - 2])
    first = jnp.zeros((1,), jnp.int32)
    final = jnp.full((1,), LAT - 1, jnp.int32)
    return jnp.concatenate([first, middle, final]).astype(jnp.int32)


def draw_band_spectrum(key, part):
    order = jax.random.permutation(jax.random.fold_in(key, 16), NBANDS).astype(jnp.int32)
    return (order % NSPEC).astype(jnp.int32)


def draw_shifts(key, part):
    both = jax.random.randint(jax.random.fold_in(key, 17), (2,), 1, WIN, dtype=jnp.int32)
    chosen = jax.random.randint(jax.random.fold_in(key, 18), (), 0, 2, dtype=jnp.int32)
    return jnp.where(jnp.arange(2, dtype=jnp.int32) == chosen, WIN - 1, both).astype(jnp.int32)


def levels(rng, dims, cuts, smallest, largest):
    level, own = 1.0, jax.random.fold_in(rng, 6)
    for axis_at, blocks in cuts:
        heights = jnp.exp(jax.random.uniform(jax.random.fold_in(own, axis_at), (blocks,), jnp.float32, smallest / len(cuts), largest / len(cuts)))
        level = level * jnp.repeat(heights, dims[axis_at] // blocks).reshape([-1 if axis == axis_at else 1 for axis in range(len(dims))])
    return level


def noise(stream_key, extent, deviation, most, cuts=(), held_as=jnp.bfloat16):
    level = levels(stream_key, extent, cuts, -0.22, 0.18) if cuts else 1.0
    entries = jax.random.normal(stream_key, extent, jnp.float32) * deviation * level
    return jnp.minimum(jnp.maximum(entries, -most), most).astype(held_as)


def setup_inputs(seed: int = 0) -> dict:
    splits = jax.random.split(jax.random.key(seed), 19)
    control = draw_control(jax.random.fold_in(splits[18], 71), 0)
    spectra = draw_spectra(jax.random.fold_in(splits[18], 71), 0)
    band_starts = draw_band_starts(jax.random.fold_in(splits[18], 71), 0)
    band_spectrum = draw_band_spectrum(jax.random.fold_in(splits[18], 71), 0)
    shifts = draw_shifts(jax.random.fold_in(splits[18], 71), 0)
    traj_start = noise(splits[5], (FIELDS, LAT, LON), 1.0, 6.0, ((1, 16), (2, 2)))
    traj_next = noise(splits[6], (FIELDS, LAT, LON), 1.0, 6.0, ((1, 16), (2, 2)))
    query_weight = noise(splits[7], (FIELDS, HEADS * HEAD), FIELDS ** -0.5, 0.75)
    key_weight = noise(splits[8], (FIELDS, HEADS * HEAD), FIELDS ** -0.5, 0.75)
    value_weight = noise(splits[9], (FIELDS, HEADS * HEAD), FIELDS ** -0.5, 0.75)
    out_weight = noise(splits[10], (HEADS * HEAD, FIELDS), (HEADS * HEAD // 4) ** -0.5, 0.75)
    head_scale = jnp.clip(jnp.exp(jax.random.uniform(splits[11], (HEADS,), jnp.float32, math.log(2.0), math.log(12.0))), 2.0, 12.0)
    innov_one = noise(splits[12], (FIELDS, LAT, LON), 1.0, 6.0, ((1, 16), (2, 2)), jnp.float32)
    innov_two = noise(splits[13], (FIELDS, LAT, LON), 1.0, 6.0, ((1, 16), (2, 2)), jnp.float32)
    obs_weight_one = draw_obs_weight_one(jax.random.fold_in(splits[18], 71), 0)
    obs_weight_two = draw_obs_weight_two(jax.random.fold_in(splits[18], 71), 0)
    grad_prev = draw_grad_prev(jax.random.fold_in(splits[18], 71), 0)
    dir_prev = noise(splits[17], (FIELDS, LAT, LON), 1.0, 6.0, ((0, 2), (1, 16)), jnp.float32)
    return {"control": control, "spectra": spectra, "band_starts": band_starts, "band_spectrum": band_spectrum, "shifts": shifts, "traj_start": traj_start, "traj_next": traj_next, "query_weight": query_weight, "key_weight": key_weight, "value_weight": value_weight, "out_weight": out_weight, "head_scale": head_scale, "innov_one": innov_one, "innov_two": innov_two, "obs_weight_one": obs_weight_one, "obs_weight_two": obs_weight_two, "grad_prev": grad_prev, "dir_prev": dir_prev}


def rounded(value):
    return lax.optimization_barrier(value.astype(jnp.bfloat16)).astype(jnp.float32)

def row_spectra(spectra, band_starts, band_spectrum):
    latitude = jnp.arange(LAT, dtype=jnp.int32)
    band_of_row = lax.optimization_barrier(jnp.sum((band_starts[None, :] <= latitude[:, None]).astype(jnp.int32), axis=1)) - 1
    chosen = band_spectrum[band_of_row]
    return jnp.transpose(spectra[chosen], (1, 0, 2))

def half_covariance(field, row_spec):
    spectral = jnp.fft.rfft(field, axis=-1)
    return jnp.fft.irfft(spectral * row_spec, n=LON, axis=-1).astype(jnp.float32)

def to_tokens(field, win):
    depth, height, width = field.shape
    blocks = field.reshape(depth, height // win, win, width // win, win)
    return blocks.transpose(1, 3, 2, 4, 0).reshape(-1, win * win, depth)

def from_tokens(tokens, height, width, win):
    depth = tokens.shape[2]
    blocks = tokens.reshape(height // win, width // win, win, win, depth)
    return blocks.transpose(4, 0, 2, 1, 3).reshape(depth, height, width)

def unit_heads(projected):
    shaped = projected.reshape(projected.shape[0], projected.shape[1], HEADS, HEAD)
    return rounded(shaped * lax.rsqrt(lax.optimization_barrier(jnp.sum(shaped * shaped, axis=-1, keepdims=True)) + 1e-06))

def attention_weights(state, query_weight, key_weight, head_scale):
    tokens = to_tokens(state, WIN).astype(jnp.float32)
    queries = unit_heads(jnp.einsum('ntc,cd->ntd', tokens, query_weight.astype(jnp.float32)))
    keys_unit = unit_heads(jnp.einsum('ntc,cd->ntd', tokens, key_weight.astype(jnp.float32)))
    scores = jnp.einsum('nthe,nshe->nhts', queries, keys_unit) * head_scale[None, :, None, None]
    raised = jnp.exp(scores)
    return rounded(raised / lax.optimization_barrier(jnp.sum(raised, axis=-1, keepdims=True)))

def window_forward(field, weights, value_weight, out_weight):
    depth, height, width = field.shape
    tokens = to_tokens(field, WIN)
    count, span = (tokens.shape[0], tokens.shape[1])
    values = rounded(jnp.einsum('ntc,cd->ntd', rounded(tokens), value_weight.astype(jnp.float32)))
    values = values.reshape(count, span, HEADS, HEAD)
    mixed = rounded(jnp.einsum('nhts,nshe->nthe', weights, values)).reshape(count, span, HEADS * HEAD)
    result = tokens + jnp.einsum('ntd,dc->ntc', mixed, out_weight.astype(jnp.float32))
    return from_tokens(result, height, width, WIN)

def window_adjoint(field, weights, value_weight, out_weight):
    depth, height, width = field.shape
    tokens = to_tokens(field, WIN)
    count, span = (tokens.shape[0], tokens.shape[1])
    upward = rounded(jnp.einsum('ntc,dc->ntd', rounded(tokens), out_weight.astype(jnp.float32)))
    upward = upward.reshape(count, span, HEADS, HEAD)
    spread_back = rounded(jnp.einsum('nhts,nthe->nshe', weights, upward)).reshape(count, span, HEADS * HEAD)
    result = tokens + jnp.einsum('ntd,cd->ntc', spread_back, value_weight.astype(jnp.float32))
    return from_tokens(result, height, width, WIN)

def apply_bands(step_fn, field, state):
    bands = LAT // WIN
    field_bands = field.reshape(FIELDS, bands, WIN, LON).transpose(1, 0, 2, 3)
    state_bands = state.reshape(FIELDS, bands, WIN, LON).transpose(1, 0, 2, 3)

    def one_band(pair):
        return step_fn(pair[0], pair[1])
    result = lax.map(one_band, (field_bands, state_bands))
    return result.transpose(1, 0, 2, 3).reshape(FIELDS, LAT, LON)

def shift_grid(field, shifts, sign):
    return jnp.roll(field, (sign * shifts[0], sign * shifts[1]), axis=(1, 2))

def reference(control, spectra, band_starts, band_spectrum, shifts, traj_start, traj_next, query_weight, key_weight, value_weight, out_weight, head_scale, innov_one, innov_two, obs_weight_one, obs_weight_two, grad_prev, dir_prev):

    def step_forward(field, state):
        weights = attention_weights(state, query_weight, key_weight, head_scale)
        return window_forward(field, weights, value_weight, out_weight)

    def step_backward(field, state):
        weights = attention_weights(state, query_weight, key_weight, head_scale)
        return window_adjoint(field, weights, value_weight, out_weight)
    row_spec = row_spectra(spectra, band_starts, band_spectrum)
    increment_start = half_covariance(control, row_spec)
    increment_one = apply_bands(step_forward, increment_start, traj_start)
    moved_state = shift_grid(traj_next, shifts, -1)
    increment_two = shift_grid(apply_bands(step_forward, shift_grid(increment_one, shifts, -1), moved_state), shifts, 1)
    misfit_one = increment_one - innov_one
    misfit_two = increment_two - innov_two
    adjoint_two = obs_weight_two * misfit_two
    carried = shift_grid(apply_bands(step_backward, shift_grid(adjoint_two, shifts, -1), moved_state), shifts, 1)
    adjoint_one = carried + obs_weight_one * misfit_one
    adjoint_start = apply_bands(step_backward, adjoint_one, traj_start)
    gradient = control + half_covariance(adjoint_start, row_spec)
    prior = jnp.sum(control * control)
    previous = jnp.sum(grad_prev * grad_prev)
    misfit = jnp.sum(obs_weight_one * misfit_one * misfit_one) + jnp.sum(obs_weight_two * misfit_two * misfit_two)
    current = jnp.sum(gradient * gradient)
    cost_value = 0.5 * (prior + misfit) / (FIELDS * LAT * LON)
    direction = -gradient + current / previous * dir_prev
    return (gradient, direction, cost_value)
```

```python
import functools
import math

import jax
import jax.numpy as jnp
import numpy as np
from jax import lax
from jax.experimental import pallas as pl
from jax.experimental.pallas import tpu as pltpu
from jax.sharding import PartitionSpec as P

WIN = 10


precise = lax.Precision.HIGHEST


def as_sent(shard):
    return jax.tree.map(lambda a: a.astype(jnp.bfloat16) if a.dtype == jnp.float32 else a, shard)


def from_behind(value, axis, steps):
    count = lax.axis_size(axis)
    pairs = [(source, (source + steps) % count) for source in range(count)]
    return lax.ppermute(value, axis, pairs)


def wave_tables(lon_len, wave_count):
    place = np.arange(lon_len)[:, None]
    wave = np.arange(wave_count)[None, :]
    angle = (place * wave % lon_len) * (2.0 * math.pi / lon_len)
    pad = -wave_count % 128
    wide = ((0, 0), (0, pad))
    table = np.concatenate([np.pad(np.cos(angle), wide), np.pad(np.sin(angle), wide)], axis=1)
    table = table.astype(np.float32)
    coarse = table.astype(jnp.bfloat16)
    fine = (table - coarse.astype(np.float32)).astype(jnp.bfloat16)
    return coarse, fine


def split_pair(value):
    coarse = lax.reduce_precision(value, 8, 7)
    return coarse.astype(jnp.bfloat16), (value - coarse).astype(jnp.bfloat16)


def half_covariance(flat, scaled, tables):
    coarse, fine = tables
    wide = np.concatenate([coarse, coarse, fine], axis=0)
    tall = np.concatenate([coarse.T, coarse.T, fine.T], axis=0)
    if flat.dtype == jnp.bfloat16:
        left = jnp.concatenate([flat, flat], axis=1)
        wide = np.concatenate([coarse, fine], axis=0)
    else:
        big, small = split_pair(flat)
        left = jnp.concatenate([big, small, big], axis=1)
    parts = jnp.dot(left, jnp.asarray(wide), preferred_element_type=jnp.float32)
    big, small = split_pair(parts * scaled)
    left = jnp.concatenate([big, small, big], axis=1)
    return jnp.dot(left, jnp.asarray(tall), preferred_element_type=jnp.float32)


SPAN = 112
GROUP = 4


def dot(a, b):
    return jnp.dot(a, b, preferred_element_type=jnp.float32)


def lay_rows(source, place):
    for r in range(WIN):
        place[r] = source[r].astype(jnp.float32).T


def take_windows(place, at, tokens):
    width = WIN * GROUP
    for r in range(WIN):
        cells = place[r, pl.ds(pl.multiple_of(at * width, 8), width), :]
        for g in range(GROUP):
            tokens[g, r * WIN : (r + 1) * WIN, :] = cells[g * WIN : (g + 1) * WIN]
    return tokens[...].reshape(GROUP * SPAN, tokens.shape[2])


def put_windows(tokens, value, strip, at, place):
    width = WIN * GROUP
    tokens[...] = value.reshape(tokens.shape)
    for r in range(WIN):
        for g in range(GROUP):
            strip[r, g * WIN : (g + 1) * WIN, :] = tokens[g, r * WIN : (r + 1) * WIN, :]
    for r in range(WIN):
        place[r, pl.ds(pl.multiple_of(at * width, 8), width), :] = strip[r]


def unit_vectors(tokens, weight, ones):
    projected = dot(tokens, weight)
    squares = dot((projected * projected).astype(jnp.bfloat16), ones)
    return projected * lax.rsqrt(squares + 1e-06)


def window_probs(query, keys, head, g):
    rows = slice(g * SPAN, (g + 1) * SPAN)
    lanes = slice(head * 64, head * 64 + 64)
    scores = lax.dot_general(
        query[rows, lanes], keys[rows, lanes], (((1,), (1,)), ((), ())),
        preferred_element_type=jnp.float32,
    )
    inside = lax.broadcasted_iota(jnp.int32, scores.shape, 1) < WIN * WIN
    raised = jnp.where(inside, jnp.exp(scores), 0.0)
    return (raised / jnp.sum(raised, axis=1, keepdims=True)).astype(jnp.bfloat16)


def mix(probs, values, mixed, heads, across):
    for g in range(GROUP):
        rows = slice(g * SPAN, (g + 1) * SPAN)
        for h in range(heads):
            lanes = slice(h * 64, h * 64 + 64)
            mixed[rows, lanes] = lax.dot_general(
                probs(g, h), values[rows, lanes], (((across,), (0,)), ((), ())),
                preferred_element_type=jnp.float32,
            )
    return mixed[...].astype(jnp.bfloat16)


def single_kernel(heads, across, state_ref, field_ref, qw, kw, inw, outw, ones, scale,
                  out_ref, place_s, place_f, tok_s, tok_f, strip, mixed):
    tok_s[...] = jnp.zeros_like(tok_s)
    lay_rows(state_ref, place_s)
    lay_rows(field_ref, place_f)

    def body(at, carry):
        tok_f[...] = jnp.zeros_like(tok_f)
        state = take_windows(place_s, at, tok_s).astype(jnp.bfloat16)
        field = take_windows(place_f, at, tok_f)
        query = (unit_vectors(state, qw[...], ones[...]) * scale[...]).astype(jnp.bfloat16)
        keys = unit_vectors(state, kw[...], ones[...]).astype(jnp.bfloat16)
        values = dot(field.astype(jnp.bfloat16), inw[...]).astype(jnp.bfloat16)
        both = mix(lambda g, h: window_probs(query, keys, h, g), values, mixed, heads, across)
        put_windows(tok_f, field + dot(both, outw[...]), strip, at, place_f)
        return carry

    lax.fori_loop(0, place_f.shape[1] // (WIN * GROUP), body, 0)
    for r in range(WIN):
        out_ref[r] = place_f[r].T.astype(out_ref.dtype)


def double_kernel(heads, state_ref, field_ref, innov_ref, obs_ref, qw, kw, vw, ow, owt, vwt,
                  ones, scale, out_ref, sum_ref, place_s, place_f, place_i, place_o,
                  tok_s, tok_f, tok_i, tok_o, strip, mixed, held):
    tok_s[...] = jnp.zeros_like(tok_s)
    tok_i[...] = jnp.zeros_like(tok_i)
    tok_o[...] = jnp.zeros_like(tok_o)
    lay_rows(state_ref, place_s)
    lay_rows(field_ref, place_f)
    lay_rows(innov_ref, place_i)
    lay_rows(obs_ref, place_o)

    @pl.when(pl.program_id(0) == 0)
    def _():
        sum_ref[...] = jnp.zeros_like(sum_ref)

    def body(at, carry):
        tok_f[...] = jnp.zeros_like(tok_f)
        state = take_windows(place_s, at, tok_s).astype(jnp.bfloat16)
        field = take_windows(place_f, at, tok_f)
        query = (unit_vectors(state, qw[...], ones[...]) * scale[...]).astype(jnp.bfloat16)
        keys = unit_vectors(state, kw[...], ones[...]).astype(jnp.bfloat16)
        values = dot(field.astype(jnp.bfloat16), vw[...]).astype(jnp.bfloat16)

        def fresh(g, h):
            probs = window_probs(query, keys, h, g)
            held[g, h] = probs
            return probs

        both = mix(fresh, values, mixed, heads, 1)
        misfit = field + dot(both, ow[...]) - take_windows(place_i, at, tok_i)
        adjoint = take_windows(place_o, at, tok_o) * misfit
        sum_ref[...] += adjoint * misfit
        upward = dot(adjoint.astype(jnp.bfloat16), owt[...]).astype(jnp.bfloat16)
        back = mix(lambda g, h: held[g, h], upward, mixed, heads, 0)
        put_windows(tok_f, adjoint + dot(back, vwt[...]), strip, at, place_f)
        return carry

    lax.fori_loop(0, place_f.shape[1] // (WIN * GROUP), body, 0)
    for r in range(WIN):
        out_ref[r] = place_f[r].T


def call_windows(kernel, arrays, small, out_dtype, with_sum, heads):
    rows, depth, width = arrays[0].shape
    f32 = jnp.float32
    block = pl.BlockSpec((WIN, depth, width), lambda i: (i, 0, 0))
    whole = [pl.BlockSpec(s.shape, lambda i: (0, 0)) for s in small]
    out_shape = [jax.ShapeDtypeStruct((rows, depth, width), out_dtype)]
    out_specs = [block]
    if with_sum:
        out_shape.append(jax.ShapeDtypeStruct((GROUP * SPAN, depth), f32))
        out_specs.append(pl.BlockSpec((GROUP * SPAN, depth), lambda i: (0, 0)))
    scratch = [pltpu.VMEM((WIN, width, depth), f32) for _ in arrays]
    scratch += [pltpu.VMEM((GROUP, SPAN, depth), f32) for _ in arrays]
    scratch += [pltpu.VMEM((WIN, WIN * GROUP, depth), f32), pltpu.VMEM((GROUP * SPAN, heads * 64), f32)]
    if with_sum:
        scratch.append(pltpu.VMEM((GROUP, heads, SPAN, SPAN), jnp.bfloat16))
    return pl.pallas_call(
        kernel,
        grid=(rows // WIN,),
        in_specs=[block] * len(arrays) + whole,
        out_shape=out_shape,
        out_specs=out_specs,
        scratch_shapes=scratch,
        compiler_params=pltpu.CompilerParams(vmem_limit_bytes=56 * 2**20),
    )(*arrays, *small)


def roll_ahead(field, shifts):
    height, depth, width = field.shape
    below = from_behind(as_sent(field[:WIN]), ("grp", "lat"), -1).astype(field.dtype)
    moved = lax.dynamic_slice_in_dim(jnp.concatenate([field, below], axis=0), shifts[0], height, 0)
    beside = from_behind(as_sent(moved[:, :, :WIN]), "lon", -1).astype(field.dtype)
    return lax.dynamic_slice_in_dim(jnp.concatenate([moved, beside], axis=2), shifts[1], width, 2)


def roll_behind(field, shifts):
    height, depth, width = field.shape
    above = from_behind(as_sent(field[height - WIN :]), ("grp", "lat"), 1).astype(field.dtype)
    moved = lax.dynamic_slice_in_dim(
        jnp.concatenate([above, field], axis=0), WIN - shifts[0], height, 0
    )
    beside = from_behind(as_sent(moved[:, :, width - WIN :]), "lon", 1).astype(field.dtype)
    return lax.dynamic_slice_in_dim(
        jnp.concatenate([beside, moved], axis=2), WIN - shifts[1], width, 2
    )


def body(
    control,
    spectra,
    band_starts,
    band_spectrum,
    shifts,
    traj_start,
    traj_next,
    query_weight,
    key_weight,
    value_weight,
    out_weight,
    head_scale,
    innov_one,
    innov_two,
    obs_weight_one,
    obs_weight_two,
    grad_prev,
    dir_prev,
):
    fields_here, row_count, lon_len = control.shape
    spec_count, wave_count = (spectra.shape[0], spectra.shape[2])
    first_row = lax.axis_index(("grp", "lat")) * row_count
    global_rows = first_row + jnp.arange(row_count, dtype=jnp.int32)
    band_of_row = (
        jnp.sum((band_starts[None, :] <= global_rows[:, None]).astype(jnp.int32), axis=1) - 1
    )
    band_hits = band_of_row[:, None] == jnp.arange(band_starts.shape[0], dtype=jnp.int32)[None, :]
    spec_of_row = jnp.sum(jnp.where(band_hits, band_spectrum[None, :], 0), axis=1)
    selector = (spec_of_row[:, None] == jnp.arange(spec_count, dtype=jnp.int32)[None, :]).astype(
        jnp.float32
    )
    row_spec = jnp.einsum(
        "rs,sfk->rfk", selector, spectra, precision=precise, preferred_element_type=jnp.float32
    )
    tables = wave_tables(lon_len, wave_count)
    wave = np.arange(wave_count)
    weight = np.where((wave == 0) | (wave == lon_len // 2), 1.0, 2.0).astype(np.float32) / lon_len
    padded = jnp.pad(row_spec * weight, ((0, 0), (0, 0), (0, -wave_count % 128)))
    scaled = jnp.concatenate([padded, padded], axis=2).reshape(row_count * fields_here, -1)
    by_row = lambda a: jnp.transpose(a, (1, 0, 2))
    heads = head_scale.shape[0]
    inner = query_weight.shape[1]
    scale = jnp.repeat(head_scale, inner // heads)[None, :]
    ones = jnp.asarray(np.kron(np.eye(heads), np.ones((64, 64))), jnp.bfloat16)
    next_state = roll_ahead(by_row(traj_next), shifts)
    innov_next = roll_ahead(by_row(innov_two), shifts)
    obs_next = roll_ahead(by_row(obs_weight_two), shifts)
    start_state = by_row(traj_start)
    prior_part = jnp.sum(control * control)
    previous_part = jnp.sum(grad_prev * grad_prev)
    control_rows = by_row(control)
    start_cycle = half_covariance(control_rows.reshape(-1, lon_len), scaled, tables)
    start_cycle = start_cycle.astype(jnp.bfloat16).reshape(row_count, fields_here, lon_len)
    increment_start = lax.all_to_all(start_cycle, "lon", split_axis=2, concat_axis=1, tiled=True)
    forward = (query_weight, key_weight, value_weight, out_weight, ones, scale)
    backward = (query_weight, key_weight, out_weight.T, value_weight.T, ones, scale)
    increment_one = call_windows(
        functools.partial(single_kernel, heads, 1),
        [start_state, increment_start], forward, jnp.float32, False, heads,
    )[0]
    carried, misfit_cells = call_windows(
        functools.partial(double_kernel, heads),
        [next_state, roll_ahead(increment_one, shifts), innov_next, obs_next],
        (query_weight, key_weight, value_weight, out_weight, out_weight.T, value_weight.T, ones, scale),
        jnp.float32, True, heads,
    )
    misfit_one = increment_one - by_row(innov_one)
    adjoint_own = by_row(obs_weight_one) * misfit_one
    misfit_part = jnp.sum(adjoint_own * misfit_one) + jnp.sum(misfit_cells)
    prior, previous, misfit = lax.psum(
        (prior_part, previous_part, misfit_part), ("grp", "lat", "lon")
    )
    adjoint_one = roll_behind(carried, shifts) + adjoint_own
    adjoint_start = call_windows(
        functools.partial(single_kernel, heads, 0),
        [start_state, adjoint_one], backward, jnp.bfloat16, False, heads,
    )[0]
    back_cycle = lax.all_to_all(adjoint_start, "lon", split_axis=1, concat_axis=2, tiled=True)
    smoothed = half_covariance(back_cycle.reshape(-1, lon_len), scaled, tables)
    gradient = control + by_row(smoothed.reshape(row_count, fields_here, lon_len))
    current = lax.psum(jnp.sum(gradient * gradient), ("grp", "lat", "lon"))
    elements = fields_here * row_count * lon_len * lax.axis_size(("grp", "lat", "lon"))
    cost_value = 0.5 * (prior + misfit) / elements
    direction = -gradient + current / previous * dir_prev
    return (gradient, direction, cost_value)


def solution(mesh):
    in_specs = (
        P("lon", ("grp", "lat"), None),
        P(None, "lon", None),
        P(),
        P(),
        P(),
        P(None, ("grp", "lat"), "lon"),
        P(None, ("grp", "lat"), "lon"),
        P(),
        P(),
        P(),
        P(),
        P(),
        P(None, ("grp", "lat"), "lon"),
        P(None, ("grp", "lat"), "lon"),
        P(None, ("grp", "lat"), "lon"),
        P(None, ("grp", "lat"), "lon"),
        P("lon", ("grp", "lat"), None),
        P("lon", ("grp", "lat"), None),
    )
    out_specs = (P("lon", ("grp", "lat"), None), P("lon", ("grp", "lat"), None), P())
    return jax.shard_map(body, mesh=mesh, in_specs=in_specs, out_specs=out_specs, check_vma=False)
```

```python
import functools
import math

import jax
import jax.numpy as jnp
import numpy as np
from jax import lax
from jax.experimental import pallas as pl
from jax.experimental.pallas import tpu as pltpu
from jax.sharding import PartitionSpec as P

WIN = 10


precise = lax.Precision.HIGHEST


def as_sent(shard):
    return jax.tree.map(lambda a: a.astype(jnp.bfloat16) if a.dtype == jnp.float32 else a, shard)


def from_behind(value, axis, steps):
    count = lax.axis_size(axis)
    pairs = [(source, (source + steps) % count) for source in range(count)]
    return lax.ppermute(value, axis, pairs)


def wave_tables(lon_len, wave_count):
    place = np.arange(lon_len)[:, None]
    wave = np.arange(wave_count)[None, :]
    angle = (place * wave % lon_len) * (2.0 * math.pi / lon_len)
    pad = -wave_count % 128
    wide = ((0, 0), (0, pad))
    table = np.concatenate([np.pad(np.cos(angle), wide), np.pad(np.sin(angle), wide)], axis=1)
    table = table.astype(np.float32)
    coarse = table.astype(jnp.bfloat16)
    fine = (table - coarse.astype(np.float32)).astype(jnp.bfloat16)
    return coarse, fine


def split_pair(value):
    coarse = lax.reduce_precision(value, 8, 7)
    return coarse.astype(jnp.bfloat16), (value - coarse).astype(jnp.bfloat16)


def half_covariance(flat, scaled, tables):
    coarse, fine = tables
    wide = np.concatenate([coarse, coarse, fine], axis=0)
    tall = np.concatenate([coarse.T, coarse.T, fine.T], axis=0)
    if flat.dtype == jnp.bfloat16:
        left = jnp.concatenate([flat, flat], axis=1)
        wide = np.concatenate([coarse, fine], axis=0)
    else:
        big, small = split_pair(flat)
        left = jnp.concatenate([big, small, big], axis=1)
    parts = jnp.dot(left, jnp.asarray(wide), preferred_element_type=jnp.float32)
    big, small = split_pair(parts * scaled)
    left = jnp.concatenate([big, small, big], axis=1)
    return jnp.dot(left, jnp.asarray(tall), preferred_element_type=jnp.float32)


SPAN = 112
GROUP = 4


def dot(a, b):
    return jnp.dot(a, b, preferred_element_type=jnp.float32)


def lay_rows(source, place):
    for r in range(WIN):
        place[r] = source[r].astype(jnp.float32).T


def take_windows(place, at, tokens):
    width = WIN * GROUP
    for r in range(WIN):
        cells = place[r, pl.ds(pl.multiple_of(at * width, 8), width), :]
        for g in range(GROUP):
            tokens[g, r * WIN : (r + 1) * WIN, :] = cells[g * WIN : (g + 1) * WIN]
    return tokens[...].reshape(GROUP * SPAN, tokens.shape[2])


def put_windows(tokens, value, strip, at, place):
    width = WIN * GROUP
    tokens[...] = value.reshape(tokens.shape)
    for r in range(WIN):
        for g in range(GROUP):
            strip[r, g * WIN : (g + 1) * WIN, :] = tokens[g, r * WIN : (r + 1) * WIN, :]
    for r in range(WIN):
        place[r, pl.ds(pl.multiple_of(at * width, 8), width), :] = strip[r]


def unit_vectors(tokens, weight, ones):
    projected = dot(tokens, weight)
    squares = dot((projected * projected).astype(jnp.bfloat16), ones)
    return projected * lax.rsqrt(squares + 1e-06)


def lone_heads(query):
    low = lax.broadcasted_iota(jnp.int32, query.shape, 1) % 128 < 64
    return jnp.where(low, query, 0.0).astype(jnp.bfloat16), jnp.where(low, 0.0, query).astype(jnp.bfloat16)


def window_probs(query, keys, head, g, across):
    rows = slice(g * SPAN, (g + 1) * SPAN)
    lanes = slice(head // 2 * 128, head // 2 * 128 + 128)
    pair = (query[head % 2][rows, lanes], keys[rows, lanes])
    scores = lax.dot_general(
        pair[1 - across], pair[across], (((1,), (1,)), ((), ())),
        preferred_element_type=jnp.float32,
    )
    inside = lax.broadcasted_iota(jnp.int32, scores.shape, across) < WIN * WIN
    raised = jnp.where(inside, jnp.exp(scores), 0.0)
    return (raised * (1.0 / jnp.sum(raised, axis=across, keepdims=True))).astype(jnp.bfloat16)


def mix(probs, values, mixed, heads, across):
    low = lax.broadcasted_iota(jnp.int32, (SPAN, 128), 1) < 64
    for g in range(GROUP):
        rows = slice(g * SPAN, (g + 1) * SPAN)
        for h in range(0, heads, 2):
            lanes = slice(h * 64, h * 64 + 128)
            first, second = (
                lax.dot_general(
                    probs(g, h + k), values[rows, lanes], (((across,), (0,)), ((), ())),
                    preferred_element_type=jnp.float32,
                )
                for k in range(2)
            )
            mixed[rows, lanes] = jnp.where(low, first, second)
    return mixed[...].astype(jnp.bfloat16)


def single_kernel(heads, across, state_ref, field_ref, qw, kw, inw, outw, ones, scale,
                  out_ref, place_s, place_f, tok_s, tok_f, strip, mixed):
    tok_s[...] = jnp.zeros_like(tok_s)
    lay_rows(state_ref, place_s)
    lay_rows(field_ref, place_f)

    def body(at, carry):
        tok_f[...] = jnp.zeros_like(tok_f)
        state = take_windows(place_s, at, tok_s).astype(jnp.bfloat16)
        field = take_windows(place_f, at, tok_f)
        query = lone_heads(unit_vectors(state, qw[...], ones[...]) * scale[...])
        keys = unit_vectors(state, kw[...], ones[...]).astype(jnp.bfloat16)
        values = dot(field.astype(jnp.bfloat16), inw[...]).astype(jnp.bfloat16)
        both = mix(lambda g, h: window_probs(query, keys, h, g, across), values, mixed, heads, 1)
        put_windows(tok_f, field + dot(both, outw[...]), strip, at, place_f)
        return carry

    lax.fori_loop(0, place_f.shape[1] // (WIN * GROUP), body, 0)
    for r in range(WIN):
        out_ref[r] = place_f[r].T.astype(out_ref.dtype)


def double_kernel(heads, state_ref, field_ref, innov_ref, obs_ref, qw, kw, vw, ow, owt, vwt,
                  ones, scale, out_ref, sum_ref, place_s, place_f, place_i, place_o,
                  tok_s, tok_f, tok_i, tok_o, strip, mixed, held):
    tok_s[...] = jnp.zeros_like(tok_s)
    tok_i[...] = jnp.zeros_like(tok_i)
    tok_o[...] = jnp.zeros_like(tok_o)
    lay_rows(state_ref, place_s)
    lay_rows(field_ref, place_f)
    lay_rows(innov_ref, place_i)
    lay_rows(obs_ref, place_o)

    @pl.when(pl.program_id(0) == 0)
    def _():
        sum_ref[...] = jnp.zeros_like(sum_ref)

    def body(at, carry):
        tok_f[...] = jnp.zeros_like(tok_f)
        state = take_windows(place_s, at, tok_s).astype(jnp.bfloat16)
        field = take_windows(place_f, at, tok_f)
        query = lone_heads(unit_vectors(state, qw[...], ones[...]) * scale[...])
        keys = unit_vectors(state, kw[...], ones[...]).astype(jnp.bfloat16)
        values = dot(field.astype(jnp.bfloat16), vw[...]).astype(jnp.bfloat16)

        def fresh(g, h):
            probs = window_probs(query, keys, h, g, 1)
            held[g, h] = probs
            return probs

        both = mix(fresh, values, mixed, heads, 1)
        misfit = field + dot(both, ow[...]) - take_windows(place_i, at, tok_i)
        adjoint = take_windows(place_o, at, tok_o) * misfit
        sum_ref[...] += adjoint * misfit
        upward = dot(adjoint.astype(jnp.bfloat16), owt[...]).astype(jnp.bfloat16)
        back = mix(lambda g, h: held[g, h], upward, mixed, heads, 0)
        put_windows(tok_f, adjoint + dot(back, vwt[...]), strip, at, place_f)
        return carry

    lax.fori_loop(0, place_f.shape[1] // (WIN * GROUP), body, 0)
    for r in range(WIN):
        out_ref[r] = place_f[r].T


def call_windows(kernel, arrays, small, out_dtype, with_sum, heads):
    rows, depth, width = arrays[0].shape
    f32 = jnp.float32
    block = pl.BlockSpec((WIN, depth, width), lambda i: (i, 0, 0))
    whole = [pl.BlockSpec(s.shape, lambda i: (0, 0)) for s in small]
    out_shape = [jax.ShapeDtypeStruct((rows, depth, width), out_dtype)]
    out_specs = [block]
    if with_sum:
        out_shape.append(jax.ShapeDtypeStruct((GROUP * SPAN, depth), f32))
        out_specs.append(pl.BlockSpec((GROUP * SPAN, depth), lambda i: (0, 0)))
    scratch = [pltpu.VMEM((WIN, width, depth), f32) for _ in arrays]
    scratch += [pltpu.VMEM((GROUP, SPAN, depth), f32) for _ in arrays]
    scratch += [pltpu.VMEM((WIN, WIN * GROUP, depth), f32), pltpu.VMEM((GROUP * SPAN, heads * 64), f32)]
    if with_sum:
        scratch.append(pltpu.VMEM((GROUP, heads, SPAN, SPAN), jnp.bfloat16))
    return pl.pallas_call(
        kernel,
        grid=(rows // WIN,),
        in_specs=[block] * len(arrays) + whole,
        out_shape=out_shape,
        out_specs=out_specs,
        scratch_shapes=scratch,
        compiler_params=pltpu.CompilerParams(vmem_limit_bytes=56 * 2**20),
    )(*arrays, *small)


def roll_ahead(field, shifts):
    height, depth, width = field.shape
    below = from_behind(as_sent(field[:WIN]), ("grp", "lat"), -1).astype(field.dtype)
    moved = lax.dynamic_slice_in_dim(jnp.concatenate([field, below], axis=0), shifts[0], height, 0)
    beside = from_behind(as_sent(moved[:, :, :WIN]), "lon", -1).astype(field.dtype)
    return lax.dynamic_slice_in_dim(jnp.concatenate([moved, beside], axis=2), shifts[1], width, 2)


def roll_behind(field, shifts):
    height, depth, width = field.shape
    above = from_behind(as_sent(field[height - WIN :]), ("grp", "lat"), 1).astype(field.dtype)
    moved = lax.dynamic_slice_in_dim(
        jnp.concatenate([above, field], axis=0), WIN - shifts[0], height, 0
    )
    beside = from_behind(as_sent(moved[:, :, width - WIN :]), "lon", 1).astype(field.dtype)
    return lax.dynamic_slice_in_dim(
        jnp.concatenate([beside, moved], axis=2), WIN - shifts[1], width, 2
    )


def body(
    control,
    spectra,
    band_starts,
    band_spectrum,
    shifts,
    traj_start,
    traj_next,
    query_weight,
    key_weight,
    value_weight,
    out_weight,
    head_scale,
    innov_one,
    innov_two,
    obs_weight_one,
    obs_weight_two,
    grad_prev,
    dir_prev,
):
    fields_here, row_count, lon_len = control.shape
    spec_count, wave_count = (spectra.shape[0], spectra.shape[2])
    first_row = lax.axis_index(("grp", "lat")) * row_count
    global_rows = first_row + jnp.arange(row_count, dtype=jnp.int32)
    band_of_row = (
        jnp.sum((band_starts[None, :] <= global_rows[:, None]).astype(jnp.int32), axis=1) - 1
    )
    band_hits = band_of_row[:, None] == jnp.arange(band_starts.shape[0], dtype=jnp.int32)[None, :]
    spec_of_row = jnp.sum(jnp.where(band_hits, band_spectrum[None, :], 0), axis=1)
    selector = (spec_of_row[:, None] == jnp.arange(spec_count, dtype=jnp.int32)[None, :]).astype(
        jnp.float32
    )
    row_spec = jnp.einsum(
        "rs,sfk->rfk", selector, spectra, precision=precise, preferred_element_type=jnp.float32
    )
    tables = wave_tables(lon_len, wave_count)
    wave = np.arange(wave_count)
    weight = np.where((wave == 0) | (wave == lon_len // 2), 1.0, 2.0).astype(np.float32) / lon_len
    padded = jnp.pad(row_spec * weight, ((0, 0), (0, 0), (0, -wave_count % 128)))
    scaled = jnp.concatenate([padded, padded], axis=2).reshape(row_count * fields_here, -1)
    by_row = lambda a: jnp.transpose(a, (1, 0, 2))
    heads = head_scale.shape[0]
    inner = query_weight.shape[1]
    scale = jnp.repeat(head_scale, inner // heads)[None, :]
    ones = jnp.asarray(np.kron(np.eye(heads), np.ones((64, 64))), jnp.bfloat16)
    next_state = roll_ahead(by_row(traj_next), shifts)
    innov_next = roll_ahead(by_row(innov_two), shifts)
    obs_next = roll_ahead(by_row(obs_weight_two), shifts)
    start_state = by_row(traj_start)
    prior_part = jnp.sum(control * control)
    previous_part = jnp.sum(grad_prev * grad_prev)
    control_rows = by_row(control)
    start_cycle = half_covariance(control_rows.reshape(-1, lon_len), scaled, tables)
    owners = lax.axis_size("lon")
    width = lon_len // owners
    blocks = jnp.stack([start_cycle[:, n * width : (n + 1) * width] for n in range(owners)])
    blocks = blocks.astype(jnp.bfloat16).reshape(owners, row_count, fields_here, width)
    blocks = lax.all_to_all(blocks, "lon", split_axis=0, concat_axis=0, tiled=True)
    increment_start = jnp.concatenate([blocks[n] for n in range(owners)], axis=1)
    forward = (query_weight, key_weight, value_weight, out_weight, ones, scale)
    backward = (query_weight, key_weight, out_weight.T, value_weight.T, ones, scale)
    increment_one = call_windows(
        functools.partial(single_kernel, heads, 1),
        [start_state, increment_start], forward, jnp.float32, False, heads,
    )[0]
    carried, misfit_cells = call_windows(
        functools.partial(double_kernel, heads),
        [next_state, roll_ahead(increment_one, shifts), innov_next, obs_next],
        (query_weight, key_weight, value_weight, out_weight, out_weight.T, value_weight.T, ones, scale),
        jnp.float32, True, heads,
    )
    misfit_one = increment_one - by_row(innov_one)
    adjoint_own = by_row(obs_weight_one) * misfit_one
    misfit_part = jnp.sum(adjoint_own * misfit_one) + jnp.sum(misfit_cells)
    prior, previous, misfit = lax.psum(
        (prior_part, previous_part, misfit_part), ("grp", "lat", "lon")
    )
    adjoint_one = roll_behind(carried, shifts) + adjoint_own
    adjoint_start = call_windows(
        functools.partial(single_kernel, heads, 0),
        [start_state, adjoint_one], backward, jnp.bfloat16, False, heads,
    )[0]
    back_cycle = lax.all_to_all(adjoint_start, "lon", split_axis=1, concat_axis=2, tiled=True)
    smoothed = half_covariance(back_cycle.reshape(-1, lon_len), scaled, tables)
    gradient = control + by_row(smoothed.reshape(row_count, fields_here, lon_len))
    current = lax.psum(jnp.sum(gradient * gradient), ("grp", "lat", "lon"))
    elements = fields_here * row_count * lon_len * lax.axis_size(("grp", "lat", "lon"))
    cost_value = 0.5 * (prior + misfit) / elements
    direction = -gradient + current / previous * dir_prev
    return (gradient, direction, cost_value)


def solution(mesh):
    in_specs = (
        P("lon", ("grp", "lat"), None),
        P(None, "lon", None),
        P(),
        P(),
        P(),
        P(None, ("grp", "lat"), "lon"),
        P(None, ("grp", "lat"), "lon"),
        P(),
        P(),
        P(),
        P(),
        P(),
        P(None, ("grp", "lat"), "lon"),
        P(None, ("grp", "lat"), "lon"),
        P(None, ("grp", "lat"), "lon"),
        P(None, ("grp", "lat"), "lon"),
        P("lon", ("grp", "lat"), None),
        P("lon", ("grp", "lat"), None),
    )
    out_specs = (P("lon", ("grp", "lat"), None), P("lon", ("grp", "lat"), None), P())
    return jax.shard_map(body, mesh=mesh, in_specs=in_specs, out_specs=out_specs, check_vma=False)
```
